128 devices in a mesh: gx: 8 (over z, core), gy: 4 (over x), gz: 4 (over y).
Axes of the slice: x: 4, y: 4, z: 4, core: 2. Of those that a mesh axis runs over, the one named last changes fastest.
Arguments:
- rhs: float32 [8, 131072], P(None, ('gx', 'gy', 'gz')), may hold values from -8 to 8
- row_order: int32 [131072], P(('gx', 'gy', 'gz')), may hold values from 0 to 1023, as said below
- x_top: float32 [2048, 131072], P(None, ('gx', 'gy', 'gz')), may hold values from -0.03125 to 0.03125
- x_outer: float32 [256, 131072], P(None, ('gx', 'gy', 'gz')), may hold values from -0.09375 to 0.09375
- x_mid: float32 [128, 131072], P(None, ('gx', 'gy', 'gz')), may hold values from -0.15625 to 0.15625
- x_leaf: float32 [960, 131072], P(None, ('gx', 'gy', 'gz')), may hold values from -0.125 to 0.125
- live_outer: int32 [8], P('gx'), may hold values from 128 to 256, as said below
- live_mid: int32 [32], P(('gx', 'gy')), may hold values from 64 to 128, as said below
- live_leaf: int32 [128], P(('gx', 'gy', 'gz')), may hold values from 480 to 960, as said below
Outputs:
- solution: float32 [8, 131072], P(None, ('gx', 'gy', 'gz'))
The draws below stay inside these ranges and needn't reach their ends.
Inputs may be any that keep to these rules, and one draw needn't show every extreme that they name: `row_order`: each aligned block of 1024 entries is a permutation of 0 to 1023. `live_outer`: some node has all 256 columns live, and some node fewer. `live_mid`: some node has all 128 columns live, and some node fewer. `live_leaf`: some device has all 960 columns live, and some device fewer.
All inputs are finite; a program needn't handle non-finite values.
Results may differ from the reference program's by a relative error of at most 0.0003.
Values sent between devices are 32-bit elements; how exact they have to be, the bound alone decides.
A program may use at most 64 MiB of HBM per device.

```python
import jax
import jax.numpy as jnp
from jax import lax

NRHS = 8
ROWS_DEV = 1024
TOP_SEP = 2048
OUTER_SEP = 256
MID_SEP = 128
LEAF_SEP = 960
ROWS = 131072
OUTER_NODES = 8
MID_NODES = 32
N_GX = 8
N_GY = 4
N_GZ = 4
DEVICES = 128


def live_counts(key, number_nodes, padded):
    draw_key, pick_key, short_key = jax.random.split(key, 3)
    values = jax.random.randint(draw_key, (number_nodes,), padded // 2, padded + 1, dtype=jnp.int32)
    chosen = jax.random.randint(pick_key, (), 0, number_nodes, dtype=jnp.int32)
    other = (chosen + 1) % number_nodes
    shorter = jax.random.randint(short_key, (), padded // 2, padded, dtype=jnp.int32)
    places = jnp.arange(number_nodes, dtype=jnp.int32)
    counts = jnp.where(places == other, shorter, values)
    return jnp.where(places == chosen, padded, counts).astype(jnp.int32)


def draw_row_order(key, part):
    key = jax.random.fold_in(key, 7)
    device_keys = jax.random.split(key, DEVICES)
    orders = jax.vmap(lambda single: jax.random.permutation(single, ROWS_DEV))(device_keys)
    return orders.astype(jnp.int32).reshape(ROWS)


def draw_live_outer(key, part):
    key = jax.random.fold_in(key, 11)
    return live_counts(key, OUTER_NODES, OUTER_SEP)


def draw_live_mid(key, part):
    key = jax.random.fold_in(key, 13)
    return live_counts(key, MID_NODES, MID_SEP)


def draw_live_leaf(key, part):
    key = jax.random.fold_in(key, 17)
    return live_counts(key, DEVICES, LEAF_SEP)


def block_scale(rng, extent, cuts, low, largest):
    def one(position, parts):
        draws = jax.random.uniform(jax.random.fold_in(jax.random.fold_in(rng, 6), position), (parts,), jnp.float32, low / len(cuts), largest / len(cuts))
        return jnp.repeat(jnp.exp(draws), extent[position] // parts).reshape((-1,) + (1,) * (len(extent) - position - 1))

    factor_of = one(*cuts[0])
    for cut in cuts[1:]:
        factor_of = factor_of * one(*cut)
    return factor_of


def gaussian(stream_key, extent, spread, most, shards=(), kind=jnp.bfloat16):
    level = block_scale(stream_key, extent, shards, -0.22, 0.18) if shards else 1.0
    array = jax.random.normal(stream_key, extent, jnp.float32) * spread * level
    return jnp.minimum(jnp.maximum(array, -most), most).astype(kind)


def setup_inputs(seed: int = 0) -> dict:
    seeds = jax.random.split(jax.random.key(seed), 10)
    return {
        "rhs": gaussian(seeds[0], (NRHS, ROWS), 1.0, 8.0, ((1, 128),), jnp.float32),
        "row_order": draw_row_order(jax.random.fold_in(seeds[9], 71), 0),
        "x_top": gaussian(seeds[2], (TOP_SEP, ROWS), (2 * (TOP_SEP * DEVICES * ROWS_DEV) ** 0.5) ** -0.5, 0.03125, ((1, 128),), jnp.float32),
        "x_outer": gaussian(seeds[3], (OUTER_SEP, ROWS), (2 * (OUTER_SEP * N_GY * N_GZ * ROWS_DEV) ** 0.5) ** -0.5, 0.09375, ((1, 128),), jnp.float32),
        "x_mid": gaussian(seeds[4], (MID_SEP, ROWS), (2 * (MID_SEP * N_GZ * ROWS_DEV) ** 0.5) ** -0.5, 0.15625, ((1, 128),), jnp.float32),
        "x_leaf": gaussian(seeds[5], (LEAF_SEP, ROWS), (2 * (LEAF_SEP * ROWS_DEV) ** 0.5) ** -0.5, 0.125, ((1, 128),), jnp.float32),
        "live_outer": draw_live_outer(jax.random.fold_in(seeds[9], 71), 0),
        "live_mid": draw_live_mid(jax.random.fold_in(seeds[9], 71), 0),
        "live_leaf": draw_live_leaf(jax.random.fold_in(seeds[9], 71), 0),
    }


def reference(rhs, row_order, x_top, x_outer, x_mid, x_leaf, live_outer, live_mid, live_leaf):
    natural = rhs.reshape(NRHS, DEVICES, ROWS_DEV)
    local_order = row_order.reshape(DEVICES, ROWS_DEV).astype(jnp.int32)
    ordered = jnp.take_along_axis(natural, local_order[None], axis=2).reshape(NRHS, ROWS)
    solution = jnp.zeros((NRHS, ROWS), jnp.float32)
    levels = ((x_top, None, 1), (x_outer, live_outer, N_GX), (x_mid, live_mid, N_GX * N_GY), (x_leaf, live_leaf, DEVICES))
    for blocks, live_count, groups in levels:
        columns = blocks.shape[0]
        grouped_rhs = ordered.reshape(NRHS, groups, ROWS // groups)
        grouped_x = blocks.reshape(columns, groups, ROWS // groups)
        separator_sums = jnp.einsum('nga,sga->gns', grouped_rhs, grouped_x, precision=lax.Precision.HIGHEST)
        if live_count is not None:
            column_mask = jnp.arange(columns, dtype=jnp.int32)[None, :] < live_count.astype(jnp.int32)[:, None]
            separator_sums = jnp.where(column_mask[:, None, :], separator_sums, jnp.float32(0.0))
        level_term = jnp.einsum('gns,sga->nga', separator_sums, grouped_x, precision=lax.Precision.HIGHEST)
        solution = solution + level_term.reshape(NRHS, ROWS)
    return solution
```

```python
import jax
import jax.numpy as jnp
from jax import lax
from jax.experimental import pallas as pl
from jax.experimental.pallas import tpu as pltpu
from jax.sharding import PartitionSpec as P

F32 = jnp.float32
BF16 = jnp.bfloat16
LANES = 128
NRHS = 8
ROWS = 1024
CHUNK = 256
TOP = 8
OUTER = 8
MID = 9
LEAF = 10
CHUNKS = 14
PLANE = 16
GX = 8
RING = 4


def halves(values):
    high = values.astype(BF16)
    return high, (values - high.astype(F32)).astype(BF16)


def stacked(values):
    high = values.astype(BF16).astype(F32)
    return jnp.concatenate([high, values - high], axis=0).astype(BF16)


def folded(values):
    return values[:NRHS] + values[NRHS:]


def permuted(rhs, order):
    out = []
    for j in range(ROWS // LANES):
        place = jnp.broadcast_to(order[j : j + 1, :], (NRHS, LANES))
        lane, block = place % LANES, place // LANES
        taken = jnp.zeros((NRHS, LANES), F32)
        for s in range(ROWS // LANES):
            source = rhs[:, s * LANES : (s + 1) * LANES]
            taken = jnp.where(block == s, jnp.take_along_axis(source, lane, axis=1), taken)
        out.append(taken)
    return jnp.concatenate(out, axis=1)


def collect(ordered, blocks):
    return lax.dot_general(ordered, blocks, (((1,), (1,)), ((), ())), preferred_element_type=F32)


def spread(weights, blocks):
    return lax.dot_general(weights, blocks, (((1,), (0,)), ((), ())), preferred_element_type=F32)


def row(pieces):
    return jnp.concatenate(pieces, axis=1)


def live(values, count):
    return jnp.where(lax.broadcasted_iota(jnp.int32, values.shape, 1) < count, values, jnp.float32(0.0))


def kernel(
    rhs_in, order_in, top_in, outer_in, mid_in, leaf_in, live_outer_in, live_mid_in, live_leaf_in, out,
    live_outer, live_mid, live_leaf,
    rhs, order, blocks, split, ordered, part, ring_send, gx_send, top_total,
    plane_recv, gx_recv, mid_recv, outer_recv, outer_send,
    load_sem, small_sem, send_sem, recv_sem,
):
    gx, gy, gz = lax.axis_index("gx"), lax.axis_index("gy"), lax.axis_index("gz")
    me = gy * RING + gz

    def load(chunk):
        return pltpu.make_async_copy(
            top_in.at[pl.ds(chunk * CHUNK, CHUNK)], blocks.at[chunk], load_sem.at[chunk]
        )

    def chunk_of(step):
        return lax.rem(me // 2 + 1 + step, TOP)

    smalls = [
        pltpu.make_async_copy(rhs_in, rhs, small_sem.at[0]),
        pltpu.make_async_copy(order_in, order, small_sem.at[1]),
        pltpu.make_async_copy(live_outer_in, live_outer, small_sem.at[2]),
        pltpu.make_async_copy(live_mid_in, live_mid, small_sem.at[3]),
        pltpu.make_async_copy(live_leaf_in, live_leaf, small_sem.at[4]),
    ]
    for copy in smalls:
        copy.start()

    @pl.loop(0, TOP)
    def _(step):
        load(chunk_of(step)).start()

    rest = [
        pltpu.make_async_copy(outer_in, blocks.at[OUTER], load_sem.at[OUTER]),
        pltpu.make_async_copy(mid_in, blocks.at[MID, pl.ds(0, 128)], load_sem.at[MID]),
    ]
    for i in range(4):
        rows = 256 if i < 3 else 192
        rest.append(
            pltpu.make_async_copy(
                leaf_in.at[pl.ds(i * CHUNK, rows)], blocks.at[LEAF + i, pl.ds(0, rows)], load_sem.at[LEAF + i]
            )
        )
    for copy in rest:
        copy.start()

    barrier = pltpu.get_barrier_semaphore()

    @pl.loop(1, PLANE)
    def _(step):
        other = lax.rem(me + step, PLANE)
        pl.semaphore_signal(barrier, inc=1, device_id={"gy": other // RING, "gz": lax.rem(other, RING)})

    @pl.loop(1, GX)
    def _(step):
        pl.semaphore_signal(barrier, inc=1, device_id={"gx": lax.rem(gx + step, GX)})

    blocks[MID, pl.ds(128, 128)] = jnp.zeros((128, ROWS), F32)
    blocks[LEAF + 3, pl.ds(192, 64)] = jnp.zeros((64, ROWS), F32)
    for copy in smalls:
        copy.wait()
    ordered[...] = stacked(permuted(rhs[...], order[...]))
    pl.semaphore_wait(barrier, PLANE - 1 + GX - 1)

    def gather_sums(chunk):
        high, low = halves(blocks[chunk])
        split[chunk, pl.ds(0, CHUNK)] = high
        split[chunk, pl.ds(CHUNK, CHUNK)] = low
        sums = folded(collect(ordered[...], high) + collect(ordered[...], low))
        part[2 * chunk] = sums[:, :LANES]
        part[2 * chunk + 1] = sums[:, LANES:]

    @pl.loop(0, TOP)
    def _(step):
        chunk = chunk_of(step)
        load(chunk).wait()
        gather_sums(chunk)
        for k in range(2):
            owner = 2 * chunk + k

            @pl.when(owner != me)
            def _():
                pltpu.make_async_remote_copy(
                    src_ref=part.at[owner],
                    dst_ref=plane_recv.at[lax.rem(me - owner + PLANE, PLANE)],
                    send_sem=send_sem.at[0],
                    recv_sem=recv_sem.at[0],
                    device_id={"gy": owner // RING, "gz": lax.rem(owner, RING)},
                ).start()

    rest[0].wait()
    gather_sums(OUTER)
    rest[1].wait()
    gather_sums(MID)
    ring_send[...] = part[pl.ds(2 * OUTER, 3)]
    for step in range(1, RING):
        pltpu.make_async_remote_copy(
            src_ref=ring_send,
            dst_ref=mid_recv.at[RING - step],
            send_sem=send_sem.at[1],
            recv_sem=recv_sem.at[1],
            device_id={"gz": lax.rem(gz + step, RING)},
        ).start()

    def leaf_chunk(i):
        rest[2 + i].wait()
        gather_sums(LEAF + i)

    leaf_chunk(0)
    leaf_chunk(1)

    def wait_for(ref, sem):
        pltpu.make_async_copy(ref, ref, sem).wait()

    wait_for(plane_recv.at[pl.ds(1, PLANE - 1)], recv_sem.at[0])
    gx_send[...] = part[me] + jnp.sum(plane_recv[pl.ds(1, PLANE - 1)], axis=0)
    for step in range(1, GX):
        pltpu.make_async_remote_copy(
            src_ref=gx_send,
            dst_ref=gx_recv.at[GX - step],
            send_sem=send_sem.at[2],
            recv_sem=recv_sem.at[2],
            device_id={"gx": lax.rem(gx + step, GX)},
        ).start()

    leaf_chunk(2)
    leaf_chunk(3)

    wait_for(mid_recv.at[pl.ds(1, RING - 1)], recv_sem.at[1])
    ring_total = ring_send[...] + jnp.sum(mid_recv[pl.ds(1, RING - 1)], axis=0)
    outer_send[...] = ring_total[:2]
    for step in range(1, RING):
        pltpu.make_async_remote_copy(
            src_ref=outer_send,
            dst_ref=outer_recv.at[RING - step],
            send_sem=send_sem.at[3],
            recv_sem=recv_sem.at[3],
            device_id={"gy": lax.rem(gy + step, RING)},
        ).start()

    wait_for(gx_recv.at[pl.ds(1, GX - 1)], recv_sem.at[2])
    top_total[me] = gx_send[...] + jnp.sum(gx_recv[pl.ds(1, GX - 1)], axis=0)

    @pl.loop(1, PLANE)
    def _(step):
        other = lax.rem(me + step, PLANE)
        pltpu.make_async_remote_copy(
            src_ref=top_total.at[me],
            dst_ref=top_total.at[me],
            send_sem=send_sem.at[4],
            recv_sem=recv_sem.at[4],
            device_id={"gy": other // RING, "gz": lax.rem(other, RING)},
        ).start()

    def spread_chunks(first, count, weights):
        doubled = []
        for i in range(count):
            both = stacked(weights[:, i * CHUNK : (i + 1) * CHUNK])
            doubled += [both, both]
        return spread(row(doubled), split[pl.ds(first, count)].reshape(count * 2 * CHUNK, ROWS))

    leaf_weights = live(row([part[2 * LEAF + i] for i in range(8)]), live_leaf[0])
    result = spread_chunks(LEAF, 4, leaf_weights)
    wait_for(outer_recv.at[pl.ds(1, RING - 1)], recv_sem.at[3])
    outer_total = outer_send[...] + jnp.sum(outer_recv[pl.ds(1, RING - 1)], axis=0)
    outer_weights = live(row([outer_total[0], outer_total[1]]), live_outer[0])
    mid_weights = live(row([ring_total[2], jnp.zeros((NRHS, LANES), F32)]), live_mid[0])
    result += spread_chunks(OUTER, 2, row([outer_weights, mid_weights]))

    wait_for(top_total.at[pl.ds(0, PLANE - 1)], recv_sem.at[4])
    result += spread_chunks(0, TOP, row([top_total[i] for i in range(PLANE)]))
    out[...] = folded(result)

    wait_for(plane_recv.at[pl.ds(1, PLANE - 1)], send_sem.at[0])
    wait_for(mid_recv.at[pl.ds(1, RING - 1)], send_sem.at[1])
    wait_for(gx_recv.at[pl.ds(1, GX - 1)], send_sem.at[2])
    wait_for(outer_recv.at[pl.ds(1, RING - 1)], send_sem.at[3])
    wait_for(top_total.at[pl.ds(0, PLANE - 1)], send_sem.at[4])


def local(rhs, row_order, x_top, x_outer, x_mid, x_leaf, live_outer, live_mid, live_leaf):
    piece = (NRHS, LANES)
    call = pl.pallas_call(
        kernel,
        out_shape=jax.ShapeDtypeStruct((NRHS, ROWS), F32),
        in_specs=[pl.BlockSpec(memory_space=pltpu.HBM)] * 6 + [pl.BlockSpec(memory_space=pl.ANY)] * 3,
        out_specs=pl.BlockSpec(memory_space=pltpu.VMEM),
        scratch_shapes=[
            pltpu.SMEM((1,), jnp.int32),
            pltpu.SMEM((1,), jnp.int32),
            pltpu.SMEM((1,), jnp.int32),
            pltpu.VMEM((NRHS, ROWS), F32),
            pltpu.VMEM((ROWS // LANES, LANES), jnp.int32),
            pltpu.VMEM((CHUNKS, CHUNK, ROWS), F32),
            pltpu.VMEM((CHUNKS, 2 * CHUNK, ROWS), BF16),
            pltpu.VMEM((2 * NRHS, ROWS), BF16),
            pltpu.VMEM((2 * CHUNKS, *piece), F32),
            pltpu.VMEM((3, *piece), F32),
            pltpu.VMEM(piece, F32),
            pltpu.VMEM((PLANE, *piece), F32),
            pltpu.VMEM((PLANE, *piece), F32),
            pltpu.VMEM((GX, *piece), F32),
            pltpu.VMEM((RING, 3, *piece), F32),
            pltpu.VMEM((RING, 2, *piece), F32),
            pltpu.VMEM((2, *piece), F32),
            pltpu.SemaphoreType.DMA((CHUNKS,)),
            pltpu.SemaphoreType.DMA((5,)),
            pltpu.SemaphoreType.DMA((5,)),
            pltpu.SemaphoreType.DMA((5,)),
        ],
        compiler_params=pltpu.CompilerParams(
            collective_id=0, has_side_effects=True, vmem_limit_bytes=48 * 1024 * 1024
        ),
        cost_estimate=pl.CostEstimate(flops=2 * 4 * 8 * 1024 * 3392, bytes_accessed=3392 * 4096, transcendentals=0),
        name="xxt",
    )
    large = (rhs, row_order.reshape(ROWS // LANES, LANES), x_top, x_outer, x_mid, x_leaf)
    large = [pltpu.with_memory_space_constraint(operand, pltpu.HBM) for operand in large]
    return call(*large, live_outer, live_mid, live_leaf)


def solution(mesh):
    return jax.shard_map(
        local,
        mesh=mesh,
        in_specs=(
            P(None, ("gx", "gy", "gz")),
            P(("gx", "gy", "gz")),
            P(None, ("gx", "gy", "gz")),
            P(None, ("gx", "gy", "gz")),
            P(None, ("gx", "gy", "gz")),
            P(None, ("gx", "gy", "gz")),
            P("gx"),
            P(("gx", "gy")),
            P(("gx", "gy", "gz")),
        ),
        out_specs=P(None, ("gx", "gy", "gz")),
        check_vma=False,
    )
```

```python
import jax
import jax.numpy as jnp
from jax import lax
from jax.experimental import pallas as pl
from jax.experimental.pallas import tpu as pltpu
from jax.sharding import PartitionSpec as P

F32 = jnp.float32
BF16 = jnp.bfloat16
LANES = 128
NRHS = 8
ROWS = 1024
WIDTH = 512
PIECES = WIDTH // LANES
TOP = 4
MIDDLE = 4
LEAF = 5
CHUNKS = 7
PLANE = 16
GX = 8
RING = 4
LATE = 9
EARLY = 2


def halves(values):
    high = values.astype(BF16)
    return high, (values - high.astype(F32)).astype(BF16)


def stacked(values):
    high = values.astype(BF16).astype(F32)
    return jnp.concatenate([high, values - high], axis=0).astype(BF16)


def folded(values):
    return values[:NRHS] + values[NRHS:]


def permuted(rhs, order):
    out = []
    for j in range(ROWS // LANES):
        place = jnp.broadcast_to(order[j : j + 1, :], (NRHS, LANES))
        lane, block = place % LANES, place // LANES
        taken = jnp.zeros((NRHS, LANES), F32)
        for s in range(ROWS // LANES):
            source = rhs[:, s * LANES : (s + 1) * LANES]
            taken = jnp.where(block == s, jnp.take_along_axis(source, lane, axis=1), taken)
        out.append(taken)
    return jnp.concatenate(out, axis=1)


def collect(ordered, blocks):
    return lax.dot_general(ordered, blocks, (((1,), (1,)), ((), ())), preferred_element_type=F32)


def spread(weights, blocks):
    return lax.dot_general(weights, blocks, (((1,), (0,)), ((), ())), preferred_element_type=F32)


def row(pieces):
    return jnp.concatenate(pieces, axis=1)


def live(values, count):
    return jnp.where(lax.broadcasted_iota(jnp.int32, values.shape, 1) < count, values, jnp.float32(0.0))


def place(piece):
    turn = PLANE - 1 - piece
    inner_y, inner_z = turn // 8, lax.rem(turn // 4, 2)
    far_y, far_z = lax.rem(turn // 2, 2), lax.rem(turn, 2)
    return far_y * (3 - 2 * inner_y) + inner_y, far_z * (3 - 2 * inner_z) + inner_z


def piece_at(gy, gz):
    inner_y, inner_z = lax.rem(gy + 1, RING) // 2, lax.rem(gz + 1, RING) // 2
    return PLANE - 1 - (inner_y * 8 + inner_z * 4 + (gy // 2) * 2 + gz // 2)


def wait_for(ref, sem):
    pltpu.make_async_copy(ref, ref, sem).wait()


def kernel(
    rhs_in, order_in, top_in, outer_in, mid_in, leaf_in, live_outer_in, live_mid_in, live_leaf_in, out,
    live_outer, live_mid, live_leaf,
    rhs, order, blocks, split, ordered, part, ring_send, gx_send, top_total, result,
    plane_recv, gx_recv, mid_recv, outer_recv, outer_send,
    load_sem, small_sem, send_sem, recv_sem, total_sem,
):
    gx, gy, gz = lax.axis_index("gx"), lax.axis_index("gy"), lax.axis_index("gz")
    me = gy * RING + gz
    mine = piece_at(gy, gz)
    smalls = [
        pltpu.make_async_copy(rhs_in, rhs, small_sem.at[0]),
        pltpu.make_async_copy(order_in, order, small_sem.at[1]),
        pltpu.make_async_copy(live_outer_in, live_outer, small_sem.at[2]),
        pltpu.make_async_copy(live_mid_in, live_mid, small_sem.at[3]),
        pltpu.make_async_copy(live_leaf_in, live_leaf, small_sem.at[4]),
    ]
    for copy in smalls:
        copy.start()
    for i in range(TOP):
        pltpu.make_async_copy(top_in.at[pl.ds(i * WIDTH, WIDTH)], blocks.at[i], load_sem.at[i]).start(priority=1)
    rest = [
        pltpu.make_async_copy(outer_in, blocks.at[MIDDLE, pl.ds(0, 256)], load_sem.at[MIDDLE]),
        pltpu.make_async_copy(mid_in, blocks.at[MIDDLE, pl.ds(256, 128)], load_sem.at[CHUNKS]),
        pltpu.make_async_copy(leaf_in.at[pl.ds(0, 512)], blocks.at[LEAF], load_sem.at[LEAF]),
        pltpu.make_async_copy(leaf_in.at[pl.ds(512, 448)], blocks.at[LEAF + 1, pl.ds(0, 448)], load_sem.at[LEAF + 1]),
    ]
    for copy in rest:
        copy.start(priority=1)

    barrier = pltpu.get_barrier_semaphore()

    @pl.loop(1, PLANE)
    def _(step):
        other = lax.rem(me + step, PLANE)
        pl.semaphore_signal(barrier, inc=1, device_id={"gy": other // RING, "gz": lax.rem(other, RING)})

    @pl.loop(1, GX)
    def _(step):
        pl.semaphore_signal(barrier, inc=1, device_id={"gx": lax.rem(gx + step, GX)})

    blocks[MIDDLE, pl.ds(384, 128)] = jnp.zeros((128, ROWS), F32)
    blocks[LEAF + 1, pl.ds(448, 64)] = jnp.zeros((64, ROWS), F32)
    for copy in smalls:
        copy.wait()
    ordered[...] = stacked(permuted(rhs[...], order[...]))

    turn = gy + gz + 2 * (gx // 2)
    late, early = turn >= LATE, turn <= EARLY
    between = jnp.logical_not(late | early)

    def enter():
        pl.semaphore_wait(barrier, PLANE - 1 + GX - 1)


    def send_piece(piece):
        to_y, to_z = place(piece)

        @pl.when(piece != mine)
        def _():
            pltpu.make_async_remote_copy(
                src_ref=part.at[piece],
                dst_ref=plane_recv.at[lax.rem(me - (to_y * RING + to_z) + PLANE, PLANE)],
                send_sem=send_sem.at[0],
                recv_sem=recv_sem.at[0],
                device_id={"gy": to_y, "gz": to_z},
            ).start()

    def send_ring():
        ring_send[...] = part[pl.ds(PIECES * MIDDLE, 3)]
        for step in range(1, RING):
            pltpu.make_async_remote_copy(
                src_ref=ring_send,
                dst_ref=mid_recv.at[RING - step],
                send_sem=send_sem.at[1],
                recv_sem=recv_sem.at[1],
                device_id={"gz": lax.rem(gz + step, RING)},
            ).start()

    def exchange_gx():
        wait_for(plane_recv.at[pl.ds(1, PLANE - 1)], recv_sem.at[0])
        gx_send[...] = part[mine] + jnp.sum(plane_recv[pl.ds(1, PLANE - 1)], axis=0)
        for step in range(1, GX):
            pltpu.make_async_remote_copy(
                src_ref=gx_send,
                dst_ref=gx_recv.at[GX - step],
                send_sem=send_sem.at[2],
                recv_sem=recv_sem.at[2],
                device_id={"gx": lax.rem(gx + step, GX)},
            ).start()

    @pl.loop(0, CHUNKS)
    def _(chunk):
        @pl.when(chunk < TOP)
        def _():
            wait_for(blocks.at[chunk], load_sem.at[chunk])

        @pl.when((chunk == MIDDLE) & between)
        def _():
            enter()
            pl.loop(0, PLANE)(send_piece)

        @pl.when((chunk == LEAF) & late)
        def _():
            exchange_gx()

        @pl.when(chunk == MIDDLE)
        def _():
            rest[0].wait()
            rest[1].wait()

        @pl.when(chunk == LEAF)
        def _():
            rest[2].wait()

        @pl.when(chunk == LEAF + 1)
        def _():
            rest[3].wait()

        high, low = halves(blocks[chunk])
        split[chunk, pl.ds(0, WIDTH)] = high
        split[chunk, pl.ds(WIDTH, WIDTH)] = low
        sums = folded(collect(ordered[...], high) + collect(ordered[...], low))
        for k in range(PIECES):
            part[PIECES * chunk + k] = sums[:, k * LANES : (k + 1) * LANES]

        @pl.when((chunk == 0) & late)
        def _():
            enter()

        @pl.when((chunk < TOP) & late)
        def _():
            for k in range(PIECES):
                send_piece(PIECES * chunk + k)

        @pl.when((chunk == MIDDLE) & jnp.logical_not(early))
        def _():
            send_ring()

    @pl.when(early)
    def _():
        enter()
        pl.loop(0, PLANE)(send_piece)
        send_ring()

    @pl.when(jnp.logical_not(late))
    def _():
        exchange_gx()

    wait_for(mid_recv.at[pl.ds(1, RING - 1)], recv_sem.at[1])
    ring_total = ring_send[...] + jnp.sum(mid_recv[pl.ds(1, RING - 1)], axis=0)
    outer_send[...] = ring_total[:2]
    for step in range(1, RING):
        pltpu.make_async_remote_copy(
            src_ref=outer_send,
            dst_ref=outer_recv.at[RING - step],
            send_sem=send_sem.at[3],
            recv_sem=recv_sem.at[3],
            device_id={"gy": lax.rem(gy + step, RING)},
        ).start()

    def twice(pieces):
        both = stacked(row(pieces))
        return row([both, both])

    leaf_weights = live(row([part[PIECES * LEAF + i] for i in range(2 * PIECES)]), live_leaf[0])
    leaf_weights = [leaf_weights[:, i * LANES : (i + 1) * LANES] for i in range(2 * PIECES)]
    result[...] = spread(
        row([twice(leaf_weights[:PIECES]), twice(leaf_weights[PIECES:])]),
        split[pl.ds(LEAF, 2)].reshape(4 * WIDTH, ROWS),
    )

    wait_for(gx_recv.at[pl.ds(1, GX - 1)], recv_sem.at[2])
    top_total[mine] = gx_send[...] + jnp.sum(gx_recv[pl.ds(1, GX - 1)], axis=0)

    def total_copy(piece, other):
        return pltpu.make_async_remote_copy(
            src_ref=top_total.at[piece],
            dst_ref=top_total.at[piece],
            send_sem=send_sem.at[4],
            recv_sem=total_sem.at[piece],
            device_id={"gy": other // RING, "gz": lax.rem(other, RING)},
        )

    @pl.loop(0, PLANE)
    def _(other):
        @pl.when(other != me)
        def _():
            total_copy(mine, other).start()

    wait_for(outer_recv.at[pl.ds(1, RING - 1)], recv_sem.at[3])
    outer_total = outer_send[...] + jnp.sum(outer_recv[pl.ds(1, RING - 1)], axis=0)
    outer_weights = live(row([outer_total[0], outer_total[1]]), live_outer[0])
    mid_weights = live(ring_total[2], live_mid[0])
    result[...] += spread(
        twice([outer_weights, mid_weights, jnp.zeros((NRHS, LANES), F32)]), split[MIDDLE]
    )

    @pl.loop(0, TOP)
    def _(chunk):
        for k in range(PIECES):
            piece = PIECES * chunk + k

            @pl.when(piece != mine)
            def _():
                total_copy(piece, me).wait_recv()

        result[...] += spread(twice([top_total[PIECES * chunk + k] for k in range(PIECES)]), split[chunk])

    out[...] = folded(result[...])

    wait_for(plane_recv.at[pl.ds(1, PLANE - 1)], send_sem.at[0])
    wait_for(mid_recv.at[pl.ds(1, RING - 1)], send_sem.at[1])
    wait_for(gx_recv.at[pl.ds(1, GX - 1)], send_sem.at[2])
    wait_for(outer_recv.at[pl.ds(1, RING - 1)], send_sem.at[3])
    wait_for(top_total.at[pl.ds(0, PLANE - 1)], send_sem.at[4])


def local(rhs, row_order, x_top, x_outer, x_mid, x_leaf, live_outer, live_mid, live_leaf):
    piece = (NRHS, LANES)
    call = pl.pallas_call(
        kernel,
        out_shape=jax.ShapeDtypeStruct((NRHS, ROWS), F32),
        in_specs=[pl.BlockSpec(memory_space=pltpu.HBM)] * 6 + [pl.BlockSpec(memory_space=pl.ANY)] * 3,
        out_specs=pl.BlockSpec(memory_space=pltpu.VMEM),
        scratch_shapes=[
            pltpu.SMEM((1,), jnp.int32),
            pltpu.SMEM((1,), jnp.int32),
            pltpu.SMEM((1,), jnp.int32),
            pltpu.VMEM((NRHS, ROWS), F32),
            pltpu.VMEM((ROWS // LANES, LANES), jnp.int32),
            pltpu.VMEM((CHUNKS, WIDTH, ROWS), F32),
            pltpu.VMEM((CHUNKS, 2 * WIDTH, ROWS), BF16),
            pltpu.VMEM((2 * NRHS, ROWS), BF16),
            pltpu.VMEM((PIECES * CHUNKS, *piece), F32),
            pltpu.VMEM((3, *piece), F32),
            pltpu.VMEM(piece, F32),
            pltpu.VMEM((PLANE, *piece), F32),
            pltpu.VMEM((2 * NRHS, ROWS), F32),
            pltpu.VMEM((PLANE, *piece), F32),
            pltpu.VMEM((GX, *piece), F32),
            pltpu.VMEM((RING, 3, *piece), F32),
            pltpu.VMEM((RING, 2, *piece), F32),
            pltpu.VMEM((2, *piece), F32),
            pltpu.SemaphoreType.DMA((CHUNKS + 1,)),
            pltpu.SemaphoreType.DMA((5,)),
            pltpu.SemaphoreType.DMA((5,)),
            pltpu.SemaphoreType.DMA((4,)),
            pltpu.SemaphoreType.DMA((PLANE,)),
        ],
        compiler_params=pltpu.CompilerParams(
            collective_id=0, has_side_effects=True, vmem_limit_bytes=48 * 1024 * 1024
        ),
        cost_estimate=pl.CostEstimate(flops=2 * 4 * 8 * 1024 * 3392, bytes_accessed=3392 * 4096, transcendentals=0),
        name="xxt",
    )
    large = (rhs, row_order.reshape(ROWS // LANES, LANES), x_top, x_outer, x_mid, x_leaf)
    large = [pltpu.with_memory_space_constraint(operand, pltpu.HBM) for operand in large]
    return call(*large, live_outer, live_mid, live_leaf)


def solution(mesh):
    return jax.shard_map(
        local,
        mesh=mesh,
        in_specs=(
            P(None, ("gx", "gy", "gz")),
            P(("gx", "gy", "gz")),
            P(None, ("gx", "gy", "gz")),
            P(None, ("gx", "gy", "gz")),
            P(None, ("gx", "gy", "gz")),
            P(None, ("gx", "gy", "gz")),
            P("gx"),
            P(("gx", "gy")),
            P(("gx", "gy", "gz")),
        ),
        out_specs=P(None, ("gx", "gy", "gz")),
        check_vma=False,
    )
```

```python
import jax
import jax.numpy as jnp
from jax import lax
from jax.experimental import pallas as pl
from jax.experimental.pallas import tpu as pltpu
from jax.sharding import PartitionSpec as P

F32 = jnp.float32
BF16 = jnp.bfloat16
LANES = 128
NRHS = 8
ROWS = 1024
WIDTH = 512
PIECES = WIDTH // LANES
HALF = PIECES // 2
TOP = 4
MIDDLE = 4
LEAF = 5
CHUNKS = 7
PLANE = 16
GX = 8
RING = 4
LATE = 9
EARLY = 1


def halves(values):
    high = values.astype(BF16)
    return high, (values - high.astype(F32)).astype(BF16)


def stacked(values):
    high = values.astype(BF16).astype(F32)
    return jnp.concatenate([high, values - high], axis=0).astype(BF16)


def folded(values):
    return values[:NRHS] + values[NRHS:]


def permuted(rhs, order):
    out = []
    for j in range(ROWS // LANES):
        place = jnp.broadcast_to(order[j : j + 1, :], (NRHS, LANES))
        lane, block = place % LANES, place // LANES
        taken = jnp.zeros((NRHS, LANES), F32)
        for s in range(ROWS // LANES):
            source = rhs[:, s * LANES : (s + 1) * LANES]
            taken = jnp.where(block == s, jnp.take_along_axis(source, lane, axis=1), taken)
        out.append(taken)
    return jnp.concatenate(out, axis=1)


def collect(ordered, blocks):
    return lax.dot_general(ordered, blocks, (((1,), (1,)), ((), ())), preferred_element_type=F32)


def spread(weights, blocks):
    return lax.dot_general(weights, blocks, (((1,), (0,)), ((), ())), preferred_element_type=F32)


def row(pieces):
    return jnp.concatenate(pieces, axis=1)


def live(values, count):
    return jnp.where(lax.broadcasted_iota(jnp.int32, values.shape, 1) < count, values, jnp.float32(0.0))


def depth_of(chunk):
    high, low = chunk // 2, lax.rem(chunk, 2)
    return 2 - low + high - 2 * high * low


def chunk_of(depth):
    high, low = depth // 2, lax.rem(depth, 2)
    return 3 - 2 * low - 3 * high + 4 * high * low


def wait_for(ref, sem):
    pltpu.make_async_copy(ref, ref, sem).wait()


def kernel(
    rhs_in, order_in, top_in, outer_in, mid_in, leaf_in, live_outer_in, live_mid_in, live_leaf_in, out,
    live_outer, live_mid, live_leaf,
    rhs, order, blocks, split, ordered, part, weights, result,
    gx_recv, plane_recv, ring_send, mid_recv, ring_total, outer_recv,
    load_sem, small_sem, send_sem, recv_sem, total_sem,
):
    gx, gy, gz = lax.axis_index("gx"), lax.axis_index("gy"), lax.axis_index("gz")
    me = gy * RING + gz
    depth, core = gx // 2, lax.rem(gx, 2)
    mine = PIECES * chunk_of(depth) + HALF * core
    smalls = [
        pltpu.make_async_copy(rhs_in, rhs, small_sem.at[0]),
        pltpu.make_async_copy(order_in, order, small_sem.at[1]),
        pltpu.make_async_copy(live_outer_in, live_outer, small_sem.at[2]),
        pltpu.make_async_copy(live_mid_in, live_mid, small_sem.at[3]),
        pltpu.make_async_copy(live_leaf_in, live_leaf, small_sem.at[4]),
    ]
    for copy in smalls:
        copy.start()
    for i in range(TOP):
        pltpu.make_async_copy(top_in.at[pl.ds(i * WIDTH, WIDTH)], blocks.at[i], load_sem.at[i]).start(priority=1)
    rest = [
        pltpu.make_async_copy(outer_in, blocks.at[MIDDLE, pl.ds(0, 256)], load_sem.at[MIDDLE]),
        pltpu.make_async_copy(mid_in, blocks.at[MIDDLE, pl.ds(256, 128)], load_sem.at[CHUNKS]),
        pltpu.make_async_copy(leaf_in.at[pl.ds(0, 512)], blocks.at[LEAF], load_sem.at[LEAF]),
        pltpu.make_async_copy(leaf_in.at[pl.ds(512, 448)], blocks.at[LEAF + 1, pl.ds(0, 448)], load_sem.at[LEAF + 1]),
    ]
    for copy in rest:
        copy.start(priority=1)

    barrier = pltpu.get_barrier_semaphore()

    @pl.loop(1, PLANE)
    def _(step):
        other = lax.rem(me + step, PLANE)
        pl.semaphore_signal(barrier, inc=1, device_id={"gy": other // RING, "gz": lax.rem(other, RING)})

    @pl.loop(1, GX)
    def _(step):
        pl.semaphore_signal(barrier, inc=1, device_id={"gx": lax.rem(gx + step, GX)})

    blocks[MIDDLE, pl.ds(384, 128)] = jnp.zeros((128, ROWS), F32)
    blocks[LEAF + 1, pl.ds(448, 64)] = jnp.zeros((64, ROWS), F32)
    for copy in smalls:
        copy.wait()
    ordered[...] = stacked(permuted(rhs[...], order[...]))

    turn = gy + gz + 2 * depth
    late, early = turn >= LATE, turn <= EARLY
    between = jnp.logical_not(late | early)

    def enter():
        pl.semaphore_wait(barrier, PLANE - 1 + GX - 1)

    def send_chunk(chunk):
        for k in range(2):
            owner = 2 * depth_of(chunk) + k

            @pl.when(owner != gx)
            def _():
                pltpu.make_async_remote_copy(
                    src_ref=part.at[pl.ds(PIECES * chunk + HALF * k, HALF)],
                    dst_ref=gx_recv.at[lax.rem(gx - owner + GX, GX)],
                    send_sem=send_sem.at[0],
                    recv_sem=recv_sem.at[0],
                    device_id={"gx": owner},
                ).start()

    def send_ring():
        ring_send[...] = part[pl.ds(PIECES * MIDDLE, 3)]
        for step in range(1, RING):
            pltpu.make_async_remote_copy(
                src_ref=ring_send,
                dst_ref=mid_recv.at[RING - step],
                send_sem=send_sem.at[1],
                recv_sem=recv_sem.at[1],
                device_id={"gz": lax.rem(gz + step, RING)},
            ).start()

    def exchange_plane():
        wait_for(gx_recv.at[pl.ds(1, GX - 1)], recv_sem.at[0])
        plane_recv[me] = part[pl.ds(mine, HALF)] + jnp.sum(gx_recv[pl.ds(1, GX - 1)], axis=0)

        @pl.loop(0, PLANE)
        def _(other):
            @pl.when(other != me)
            def _():
                pltpu.make_async_remote_copy(
                    src_ref=plane_recv.at[me],
                    dst_ref=plane_recv.at[me],
                    send_sem=send_sem.at[2],
                    recv_sem=recv_sem.at[2],
                    device_id={"gy": other // RING, "gz": lax.rem(other, RING)},
                ).start()

    def exchange_gy():
        wait_for(mid_recv.at[pl.ds(1, RING - 1)], recv_sem.at[1])
        ring_total[...] = ring_send[...] + jnp.sum(mid_recv[pl.ds(1, RING - 1)], axis=0)
        for step in range(1, RING):
            pltpu.make_async_remote_copy(
                src_ref=ring_total.at[pl.ds(0, 2)],
                dst_ref=outer_recv.at[RING - step],
                send_sem=send_sem.at[3],
                recv_sem=recv_sem.at[3],
                device_id={"gy": lax.rem(gy + step, RING)},
            ).start()

    def after_top():
        exchange_plane()
        pl.when(depth < RING - 1)(exchange_gy)

    @pl.loop(0, CHUNKS)
    def _(chunk):
        @pl.when(chunk < TOP)
        def _():
            wait_for(blocks.at[chunk], load_sem.at[chunk])

        @pl.when((chunk == MIDDLE) & between)
        def _():
            enter()
            pl.loop(0, TOP)(send_chunk)

        @pl.when((chunk == LEAF) & jnp.logical_not(early))
        def _():
            after_top()

        @pl.when(chunk == MIDDLE)
        def _():
            rest[0].wait()
            rest[1].wait()

        @pl.when(chunk == LEAF)
        def _():
            rest[2].wait()

        @pl.when(chunk == LEAF + 1)
        def _():
            rest[3].wait()

        high, low = halves(blocks[chunk])
        split[chunk, pl.ds(0, WIDTH)] = high
        split[chunk, pl.ds(WIDTH, WIDTH)] = low
        sums = folded(collect(ordered[...], high) + collect(ordered[...], low))
        for k in range(PIECES):
            part[PIECES * chunk + k] = sums[:, k * LANES : (k + 1) * LANES]

        @pl.when((chunk == 0) & late)
        def _():
            enter()

        @pl.when((chunk < TOP) & late)
        def _():
            send_chunk(chunk)

        @pl.when((chunk == MIDDLE) & jnp.logical_not(early))
        def _():
            send_ring()

    @pl.when(early)
    def _():
        enter()
        pl.loop(0, TOP)(send_chunk)
        send_ring()
        after_top()

    def twice(pieces):
        both = stacked(row(pieces))
        return row([both, both])

    leaf_weights = live(row([part[PIECES * LEAF + i] for i in range(2 * PIECES)]), live_leaf[0])
    leaf_weights = [leaf_weights[:, i * LANES : (i + 1) * LANES] for i in range(2 * PIECES)]
    result[...] = spread(
        row([twice(leaf_weights[:PIECES]), twice(leaf_weights[PIECES:])]),
        split[pl.ds(LEAF, 2)].reshape(4 * WIDTH, ROWS),
    )

    def total_copy(owner, other):
        piece = PIECES * chunk_of(owner // 2) + HALF * lax.rem(owner, 2)
        pieces = weights.at[pl.ds(piece, HALF)]
        return pltpu.make_async_remote_copy(
            src_ref=pieces,
            dst_ref=pieces,
            send_sem=send_sem.at[4],
            recv_sem=total_sem.at[owner],
            device_id={"gx": other},
        )

    def exchange_total():
        wait_for(plane_recv.at[pl.ds(0, PLANE - 1)], recv_sem.at[2])
        weights[pl.ds(mine, HALF)] = jnp.sum(plane_recv[...], axis=0)
        for other in range(GX):

            @pl.when(gx != other)
            def _():
                total_copy(gx, other).start()

    first = 1 - (depth + RING - 1) // RING

    @pl.loop(0, TOP + 1)
    def _(step):
        after = [(step + TOP - k) // TOP for k in range(TOP + 1)]
        chunk = step + first * (TOP - after[1] - 2 * after[2] - after[3] + 2 * after[4] - step)

        @pl.when(((step == 0) & (depth > 0)) | ((step == 1) & (depth == 0)))
        def _():
            exchange_total()

        @pl.when((step == 0) & (depth == RING - 1))
        def _():
            exchange_gy()

        @pl.when(chunk < TOP)
        def _():
            for k in range(2):
                owner = 2 * depth_of(chunk) + k

                @pl.when(owner != gx)
                def _():
                    total_copy(owner, gx).wait_recv()

        @pl.when(chunk == MIDDLE)
        def _():
            wait_for(outer_recv.at[pl.ds(1, RING - 1)], recv_sem.at[3])
            outer_total = ring_total[pl.ds(0, 2)] + jnp.sum(outer_recv[pl.ds(1, RING - 1)], axis=0)
            outer_weights = live(row([outer_total[0], outer_total[1]]), live_outer[0])
            weights[PIECES * MIDDLE] = outer_weights[:, :LANES]
            weights[PIECES * MIDDLE + 1] = outer_weights[:, LANES:]
            weights[PIECES * MIDDLE + 2] = live(ring_total[2], live_mid[0])
            weights[PIECES * MIDDLE + 3] = jnp.zeros((NRHS, LANES), F32)

        result[...] += spread(twice([weights[PIECES * chunk + k] for k in range(PIECES)]), split[chunk])

    out[...] = folded(result[...])

    wait_for(gx_recv.at[pl.ds(1, GX - 1)], send_sem.at[0])
    wait_for(mid_recv.at[pl.ds(1, RING - 1)], send_sem.at[1])
    wait_for(plane_recv.at[pl.ds(0, PLANE - 1)], send_sem.at[2])
    wait_for(outer_recv.at[pl.ds(1, RING - 1)], send_sem.at[3])
    wait_for(gx_recv.at[pl.ds(1, GX - 1)], send_sem.at[4])


def local(rhs, row_order, x_top, x_outer, x_mid, x_leaf, live_outer, live_mid, live_leaf):
    piece = (NRHS, LANES)
    call = pl.pallas_call(
        kernel,
        out_shape=jax.ShapeDtypeStruct((NRHS, ROWS), F32),
        in_specs=[pl.BlockSpec(memory_space=pltpu.HBM)] * 6 + [pl.BlockSpec(memory_space=pl.ANY)] * 3,
        out_specs=pl.BlockSpec(memory_space=pltpu.VMEM),
        scratch_shapes=[
            pltpu.SMEM((1,), jnp.int32),
            pltpu.SMEM((1,), jnp.int32),
            pltpu.SMEM((1,), jnp.int32),
            pltpu.VMEM((NRHS, ROWS), F32),
            pltpu.VMEM((ROWS // LANES, LANES), jnp.int32),
            pltpu.VMEM((CHUNKS, WIDTH, ROWS), F32),
            pltpu.VMEM((CHUNKS, 2 * WIDTH, ROWS), BF16),
            pltpu.VMEM((2 * NRHS, ROWS), BF16),
            pltpu.VMEM((PIECES * CHUNKS, *piece), F32),
            pltpu.VMEM((PIECES * (TOP + 1), *piece), F32),
            pltpu.VMEM((2 * NRHS, ROWS), F32),
            pltpu.VMEM((GX, HALF, *piece), F32),
            pltpu.VMEM((PLANE, HALF, *piece), F32),
            pltpu.VMEM((3, *piece), F32),
            pltpu.VMEM((RING, 3, *piece), F32),
            pltpu.VMEM((3, *piece), F32),
            pltpu.VMEM((RING, 2, *piece), F32),
            pltpu.SemaphoreType.DMA((CHUNKS + 1,)),
            pltpu.SemaphoreType.DMA((5,)),
            pltpu.SemaphoreType.DMA((5,)),
            pltpu.SemaphoreType.DMA((4,)),
            pltpu.SemaphoreType.DMA((GX,)),
        ],
        compiler_params=pltpu.CompilerParams(
            collective_id=0, has_side_effects=True, vmem_limit_bytes=48 * 1024 * 1024
        ),
        cost_estimate=pl.CostEstimate(flops=2 * 4 * 8 * 1024 * 3392, bytes_accessed=3392 * 4096, transcendentals=0),
        name="xxt",
    )
    large = (rhs, row_order.reshape(ROWS // LANES, LANES), x_top, x_outer, x_mid, x_leaf)
    large = [pltpu.with_memory_space_constraint(operand, pltpu.HBM) for operand in large]
    return call(*large, live_outer, live_mid, live_leaf)


def solution(mesh):
    return jax.shard_map(
        local,
        mesh=mesh,
        in_specs=(
            P(None, ("gx", "gy", "gz")),
            P(("gx", "gy", "gz")),
            P(None, ("gx", "gy", "gz")),
            P(None, ("gx", "gy", "gz")),
            P(None, ("gx", "gy", "gz")),
            P(None, ("gx", "gy", "gz")),
            P("gx"),
            P(("gx", "gy")),
            P(("gx", "gy", "gz")),
        ),
        out_specs=P(None, ("gx", "gy", "gz")),
        check_vma=False,
    )
```

```python
import jax
import jax.numpy as jnp
from jax import lax
from jax.experimental import pallas as pl
from jax.experimental.pallas import tpu as pltpu
from jax.sharding import PartitionSpec as P

F32 = jnp.float32
BF16 = jnp.bfloat16
LANES = 128
NRHS = 8
ROWS = 1024
WIDTH = 512
PIECES = WIDTH // LANES
HALF = PIECES // 2
SIDE = WIDTH // 2
TOP = 4
MIDDLE = 4
LEAF = 5
CHUNKS = 7
PLANE = 16
GX = 8
RING = 4
LATE = 9
EARLY = 1


def halves(values):
    high = values.astype(BF16)
    return high, (values - high.astype(F32)).astype(BF16)


def stacked(values):
    high = values.astype(BF16).astype(F32)
    return jnp.concatenate([high, values - high], axis=0).astype(BF16)


def folded(values):
    return values[:NRHS] + values[NRHS:]


def permuted(rhs, order):
    out = []
    for j in range(ROWS // LANES):
        place = jnp.broadcast_to(order[j : j + 1, :], (NRHS, LANES))
        lane, block = place % LANES, place // LANES
        taken = jnp.zeros((NRHS, LANES), F32)
        for s in range(ROWS // LANES):
            source = rhs[:, s * LANES : (s + 1) * LANES]
            taken = jnp.where(block == s, jnp.take_along_axis(source, lane, axis=1), taken)
        out.append(taken)
    return jnp.concatenate(out, axis=1)


def collect(ordered, blocks):
    return lax.dot_general(ordered, blocks, (((1,), (1,)), ((), ())), preferred_element_type=F32)


def spread(weights, blocks):
    return lax.dot_general(weights, blocks, (((1,), (0,)), ((), ())), preferred_element_type=F32)


def row(pieces):
    return jnp.concatenate(pieces, axis=1)


def live(values, count):
    return jnp.where(lax.broadcasted_iota(jnp.int32, values.shape, 1) < count, values, jnp.float32(0.0))


def depth_of(chunk):
    high, low = chunk // 2, lax.rem(chunk, 2)
    return 2 - low + high - 2 * high * low


def chunk_of(depth):
    high, low = depth // 2, lax.rem(depth, 2)
    return 3 - 2 * low - 3 * high + 4 * high * low


def wait_for(ref, sem):
    pltpu.make_async_copy(ref, ref, sem).wait()


def kernel(
    rhs_in, order_in, top_in, outer_in, mid_in, leaf_in, live_outer_in, live_mid_in, live_leaf_in, out,
    live_outer, live_mid, live_leaf,
    rhs, order, blocks, split, ordered, part, weights, result,
    gx_recv, plane_recv, ring_send, mid_recv, ring_total, outer_recv,
    load_sem, small_sem, send_sem, recv_sem, total_sem,
):
    gx, gy, gz = lax.axis_index("gx"), lax.axis_index("gy"), lax.axis_index("gz")
    me = gy * RING + gz
    depth, core = gx // 2, lax.rem(gx, 2)
    mine = PIECES * chunk_of(depth) + HALF * core
    smalls = [
        pltpu.make_async_copy(rhs_in, rhs, small_sem.at[0]),
        pltpu.make_async_copy(order_in, order, small_sem.at[1]),
        pltpu.make_async_copy(live_outer_in, live_outer, small_sem.at[2]),
        pltpu.make_async_copy(live_mid_in, live_mid, small_sem.at[3]),
        pltpu.make_async_copy(live_leaf_in, live_leaf, small_sem.at[4]),
    ]
    for copy in smalls:
        copy.start()
    edges = [
        pltpu.make_async_copy(
            top_in.at[pl.ds(i * SIDE, SIDE)], blocks.at[0, pl.ds(i * SIDE, SIDE)], load_sem.at[CHUNKS + 1 + i]
        )
        for i in range(2)
    ]
    for copy in edges:
        copy.start(priority=1)
    for i in range(1, TOP):
        pltpu.make_async_copy(top_in.at[pl.ds(i * WIDTH, WIDTH)], blocks.at[i], load_sem.at[i]).start(priority=1)
    rest = [
        pltpu.make_async_copy(outer_in, blocks.at[MIDDLE, pl.ds(0, 256)], load_sem.at[MIDDLE]),
        pltpu.make_async_copy(mid_in, blocks.at[MIDDLE, pl.ds(256, 128)], load_sem.at[CHUNKS]),
        pltpu.make_async_copy(leaf_in.at[pl.ds(0, 512)], blocks.at[LEAF], load_sem.at[LEAF]),
        pltpu.make_async_copy(leaf_in.at[pl.ds(512, 448)], blocks.at[LEAF + 1, pl.ds(0, 448)], load_sem.at[LEAF + 1]),
    ]
    for copy in rest:
        copy.start(priority=1)

    barrier = pltpu.get_barrier_semaphore()

    @pl.loop(1, PLANE)
    def _(step):
        other = lax.rem(me + step, PLANE)
        pl.semaphore_signal(barrier, inc=1, device_id={"gy": other // RING, "gz": lax.rem(other, RING)})

    @pl.loop(1, GX)
    def _(step):
        pl.semaphore_signal(barrier, inc=1, device_id={"gx": lax.rem(gx + step, GX)})

    blocks[MIDDLE, pl.ds(384, 128)] = jnp.zeros((128, ROWS), F32)
    blocks[LEAF + 1, pl.ds(448, 64)] = jnp.zeros((64, ROWS), F32)
    for copy in smalls:
        copy.wait()
    ordered[...] = stacked(permuted(rhs[...], order[...]))

    turn = gy + gz + 2 * depth
    late, early = turn >= LATE, turn <= EARLY
    between = jnp.logical_not(late | early)
    last = depth == RING - 1

    def enter():
        pl.semaphore_wait(barrier, PLANE - 1 + GX - 1)

    def send_half(chunk, k):
        owner = 2 * depth_of(chunk) + k

        @pl.when(owner != gx)
        def _():
            pltpu.make_async_remote_copy(
                src_ref=part.at[pl.ds(PIECES * chunk + HALF * k, HALF)],
                dst_ref=gx_recv.at[lax.rem(gx - owner + GX, GX)],
                send_sem=send_sem.at[0],
                recv_sem=recv_sem.at[0],
                device_id={"gx": owner},
            ).start()

    def send_chunk(chunk):
        send_half(chunk, 0)
        send_half(chunk, 1)

    def send_ring():
        ring_send[...] = part[pl.ds(PIECES * MIDDLE, 3)]
        for step in range(1, RING):
            pltpu.make_async_remote_copy(
                src_ref=ring_send,
                dst_ref=mid_recv.at[RING - step],
                send_sem=send_sem.at[1],
                recv_sem=recv_sem.at[1],
                device_id={"gz": lax.rem(gz + step, RING)},
            ).start()

    def exchange_plane():
        wait_for(gx_recv.at[pl.ds(1, GX - 1)], recv_sem.at[0])
        plane_recv[me] = part[pl.ds(mine, HALF)] + jnp.sum(gx_recv[pl.ds(1, GX - 1)], axis=0)

        @pl.loop(0, PLANE)
        def _(other):
            @pl.when(other != me)
            def _():
                pltpu.make_async_remote_copy(
                    src_ref=plane_recv.at[me],
                    dst_ref=plane_recv.at[me],
                    send_sem=send_sem.at[2],
                    recv_sem=recv_sem.at[2],
                    device_id={"gy": other // RING, "gz": lax.rem(other, RING)},
                ).start()

    def exchange_gy():
        wait_for(mid_recv.at[pl.ds(1, RING - 1)], recv_sem.at[1])
        ring_total[...] = ring_send[...] + jnp.sum(mid_recv[pl.ds(1, RING - 1)], axis=0)
        for step in range(1, RING):
            pltpu.make_async_remote_copy(
                src_ref=ring_total.at[pl.ds(0, 2)],
                dst_ref=outer_recv.at[RING - step],
                send_sem=send_sem.at[3],
                recv_sem=recv_sem.at[3],
                device_id={"gy": lax.rem(gy + step, RING)},
            ).start()

    def after_top():
        exchange_plane()
        pl.when(depth < RING - 1)(exchange_gy)

    def gather_sums(chunk, start, width):
        high, low = halves(blocks[chunk, pl.ds(start, width)])
        split[chunk, pl.ds(start, width)] = high
        split[chunk, pl.ds(WIDTH + start, width)] = low
        sums = folded(collect(ordered[...], high) + collect(ordered[...], low))
        for k in range(width // LANES):
            part[PIECES * chunk + start // LANES + k] = sums[:, k * LANES : (k + 1) * LANES]

    edges[0].wait()
    gather_sums(0, 0, SIDE)

    @pl.loop(0, CHUNKS)
    def _(chunk):
        @pl.when((chunk > 0) & (chunk < TOP))
        def _():
            wait_for(blocks.at[chunk], load_sem.at[chunk])

        @pl.when((chunk == MIDDLE) & between)
        def _():
            enter()
            pl.loop(0, TOP)(send_chunk)

        @pl.when((chunk == MIDDLE) & last)
        def _():
            exchange_plane()

        @pl.when((chunk == LEAF) & jnp.logical_not(early | last))
        def _():
            after_top()

        @pl.when(chunk == MIDDLE)
        def _():
            rest[0].wait()
            rest[1].wait()

        @pl.when(chunk == LEAF)
        def _():
            rest[2].wait()

        @pl.when(chunk == LEAF + 1)
        def _():
            rest[3].wait()

        @pl.when(chunk > 0)
        def _():
            gather_sums(chunk, 0, WIDTH)

        @pl.when(chunk == 0)
        def _():
            edges[1].wait()
            gather_sums(0, SIDE, SIDE)

        @pl.when((chunk == 0) & late)
        def _():
            enter()

        @pl.when((chunk < TOP) & late)
        def _():
            send_chunk(chunk)

        @pl.when((chunk == MIDDLE) & jnp.logical_not(early))
        def _():
            send_ring()

    @pl.when(early)
    def _():
        enter()
        pl.loop(0, TOP)(send_chunk)
        send_ring()
        after_top()

    def twice(pieces):
        both = stacked(row(pieces))
        return row([both, both])

    leaf_weights = live(row([part[PIECES * LEAF + i] for i in range(2 * PIECES)]), live_leaf[0])
    leaf_weights = [leaf_weights[:, i * LANES : (i + 1) * LANES] for i in range(2 * PIECES)]
    result[...] = spread(
        row([twice(leaf_weights[:PIECES]), twice(leaf_weights[PIECES:])]),
        split[pl.ds(LEAF, 2)].reshape(4 * WIDTH, ROWS),
    )

    def total_copy(owner, other):
        piece = PIECES * chunk_of(owner // 2) + HALF * lax.rem(owner, 2)
        pieces = weights.at[pl.ds(piece, HALF)]
        return pltpu.make_async_remote_copy(
            src_ref=pieces,
            dst_ref=pieces,
            send_sem=send_sem.at[4],
            recv_sem=total_sem.at[owner],
            device_id={"gx": other},
        )

    def exchange_total():
        wait_for(plane_recv.at[pl.ds(0, PLANE - 1)], recv_sem.at[2])
        weights[pl.ds(mine, HALF)] = jnp.sum(plane_recv[...], axis=0)
        for other in range(GX):

            @pl.when(gx != other)
            def _():
                total_copy(gx, other).start()

    first = 1 - (depth + RING - 1) // RING

    @pl.loop(0, TOP + 1)
    def _(step):
        after = [(step + TOP - k) // TOP for k in range(TOP + 1)]
        chunk = step + first * (TOP - after[1] - 3 * after[2] + after[3] + after[4] - step)

        @pl.when(((step == 0) & (depth > 0)) | ((step == 1) & (depth == 0)))
        def _():
            exchange_total()

        @pl.when((step == 0) & (depth == RING - 1))
        def _():
            exchange_gy()

        @pl.when(chunk < TOP)
        def _():
            for k in range(2):
                owner = 2 * depth_of(chunk) + k

                @pl.when(owner != gx)
                def _():
                    total_copy(owner, gx).wait_recv()

        @pl.when(chunk == MIDDLE)
        def _():
            wait_for(outer_recv.at[pl.ds(1, RING - 1)], recv_sem.at[3])
            outer_total = ring_total[pl.ds(0, 2)] + jnp.sum(outer_recv[pl.ds(1, RING - 1)], axis=0)
            outer_weights = live(row([outer_total[0], outer_total[1]]), live_outer[0])
            weights[PIECES * MIDDLE] = outer_weights[:, :LANES]
            weights[PIECES * MIDDLE + 1] = outer_weights[:, LANES:]
            weights[PIECES * MIDDLE + 2] = live(ring_total[2], live_mid[0])
            weights[PIECES * MIDDLE + 3] = jnp.zeros((NRHS, LANES), F32)

        result[...] += spread(twice([weights[PIECES * chunk + k] for k in range(PIECES)]), split[chunk])

    out[...] = folded(result[...])

    wait_for(gx_recv.at[pl.ds(1, GX - 1)], send_sem.at[0])
    wait_for(mid_recv.at[pl.ds(1, RING - 1)], send_sem.at[1])
    wait_for(plane_recv.at[pl.ds(0, PLANE - 1)], send_sem.at[2])
    wait_for(outer_recv.at[pl.ds(1, RING - 1)], send_sem.at[3])
    wait_for(gx_recv.at[pl.ds(1, GX - 1)], send_sem.at[4])


def local(rhs, row_order, x_top, x_outer, x_mid, x_leaf, live_outer, live_mid, live_leaf):
    piece = (NRHS, LANES)
    call = pl.pallas_call(
        kernel,
        out_shape=jax.ShapeDtypeStruct((NRHS, ROWS), F32),
        in_specs=[pl.BlockSpec(memory_space=pltpu.HBM)] * 6 + [pl.BlockSpec(memory_space=pl.ANY)] * 3,
        out_specs=pl.BlockSpec(memory_space=pltpu.VMEM),
        scratch_shapes=[
            pltpu.SMEM((1,), jnp.int32),
            pltpu.SMEM((1,), jnp.int32),
            pltpu.SMEM((1,), jnp.int32),
            pltpu.VMEM((NRHS, ROWS), F32),
            pltpu.VMEM((ROWS // LANES, LANES), jnp.int32),
            pltpu.VMEM((CHUNKS, WIDTH, ROWS), F32),
            pltpu.VMEM((CHUNKS, 2 * WIDTH, ROWS), BF16),
            pltpu.VMEM((2 * NRHS, ROWS), BF16),
            pltpu.VMEM((PIECES * CHUNKS, *piece), F32),
            pltpu.VMEM((PIECES * (TOP + 1), *piece), F32),
            pltpu.VMEM((2 * NRHS, ROWS), F32),
            pltpu.VMEM((GX, HALF, *piece), F32),
            pltpu.VMEM((PLANE, HALF, *piece), F32),
            pltpu.VMEM((3, *piece), F32),
            pltpu.VMEM((RING, 3, *piece), F32),
            pltpu.VMEM((3, *piece), F32),
            pltpu.VMEM((RING, 2, *piece), F32),
            pltpu.SemaphoreType.DMA((CHUNKS + 3,)),
            pltpu.SemaphoreType.DMA((5,)),
            pltpu.SemaphoreType.DMA((5,)),
            pltpu.SemaphoreType.DMA((4,)),
            pltpu.SemaphoreType.DMA((GX,)),
        ],
        compiler_params=pltpu.CompilerParams(
            collective_id=0, has_side_effects=True, vmem_limit_bytes=48 * 1024 * 1024
        ),
        cost_estimate=pl.CostEstimate(flops=2 * 4 * 8 * 1024 * 3392, bytes_accessed=3392 * 4096, transcendentals=0),
        name="xxt",
    )
    large = (rhs, row_order.reshape(ROWS // LANES, LANES), x_top, x_outer, x_mid, x_leaf)
    large = [pltpu.with_memory_space_constraint(operand, pltpu.HBM) for operand in large]
    return call(*large, live_outer, live_mid, live_leaf)


def solution(mesh):
    return jax.shard_map(
        local,
        mesh=mesh,
        in_specs=(
            P(None, ("gx", "gy", "gz")),
            P(("gx", "gy", "gz")),
            P(None, ("gx", "gy", "gz")),
            P(None, ("gx", "gy", "gz")),
            P(None, ("gx", "gy", "gz")),
            P(None, ("gx", "gy", "gz")),
            P("gx"),
            P(("gx", "gy")),
            P(("gx", "gy", "gz")),
        ),
        out_specs=P(None, ("gx", "gy", "gz")),
        check_vma=False,
    )
```

```python
import jax
import jax.numpy as jnp
from jax import lax
from jax.experimental import pallas as pl
from jax.experimental.pallas import tpu as pltpu
from jax.sharding import PartitionSpec as P

F32 = jnp.float32
BF16 = jnp.bfloat16
LANES = 128
NRHS = 8
ROWS = 1024
WIDTH = 512
PIECES = WIDTH // LANES
HALF = PIECES // 2
SIDE = WIDTH // 2
TOP = 4
MIDDLE = 4
LEAF = 5
CHUNKS = 7
PLANE = 16
GX = 8
RING = 4
LATE = 5
LATEST = 11
EARLY = 1


def halves(values):
    high = values.astype(BF16)
    return high, (values - high.astype(F32)).astype(BF16)


def stacked(values):
    high = values.astype(BF16).astype(F32)
    return jnp.concatenate([high, values - high], axis=0).astype(BF16)


def folded(values):
    return values[:NRHS] + values[NRHS:]


def permuted(rhs, order):
    out = []
    for j in range(ROWS // LANES):
        place = jnp.broadcast_to(order[j : j + 1, :], (NRHS, LANES))
        lane, block = place % LANES, place // LANES
        taken = jnp.zeros((NRHS, LANES), F32)
        for s in range(ROWS // LANES):
            source = rhs[:, s * LANES : (s + 1) * LANES]
            taken = jnp.where(block == s, jnp.take_along_axis(source, lane, axis=1), taken)
        out.append(taken)
    return jnp.concatenate(out, axis=1)


def collect(ordered, blocks):
    return lax.dot_general(ordered, blocks, (((1,), (1,)), ((), ())), preferred_element_type=F32)


def spread(weights, blocks):
    return lax.dot_general(weights, blocks, (((1,), (0,)), ((), ())), preferred_element_type=F32)


def row(pieces):
    return jnp.concatenate(pieces, axis=1)


def live(values, count):
    return jnp.where(lax.broadcasted_iota(jnp.int32, values.shape, 1) < count, values, jnp.float32(0.0))


def depth_of(chunk):
    high, low = chunk // 2, lax.rem(chunk, 2)
    return 2 - low + high - 2 * high * low


def chunk_of(depth):
    high, low = depth // 2, lax.rem(depth, 2)
    return 3 - 2 * low - 3 * high + 4 * high * low


def wait_for(ref, sem):
    pltpu.make_async_copy(ref, ref, sem).wait()


def kernel(
    rhs_in, order_in, top_in, outer_in, mid_in, leaf_in, live_outer_in, live_mid_in, live_leaf_in, out,
    live_outer, live_mid, live_leaf,
    rhs, order, blocks, split, ordered, part, weights, result,
    gx_recv, plane_recv, ring_send, mid_recv, ring_total, outer_recv,
    load_sem, small_sem, send_sem, recv_sem, total_sem,
):
    gx, gy, gz = lax.axis_index("gx"), lax.axis_index("gy"), lax.axis_index("gz")
    me = gy * RING + gz
    depth, core = gx // 2, lax.rem(gx, 2)
    mine = PIECES * chunk_of(depth) + HALF * core
    smalls = [
        pltpu.make_async_copy(rhs_in, rhs, small_sem.at[0]),
        pltpu.make_async_copy(order_in, order, small_sem.at[1]),
        pltpu.make_async_copy(live_outer_in, live_outer, small_sem.at[2]),
        pltpu.make_async_copy(live_mid_in, live_mid, small_sem.at[3]),
        pltpu.make_async_copy(live_leaf_in, live_leaf, small_sem.at[4]),
    ]
    for copy in smalls:
        copy.start()
    edges = [
        pltpu.make_async_copy(
            top_in.at[pl.ds(i * SIDE, SIDE)], blocks.at[0, pl.ds(i * SIDE, SIDE)], load_sem.at[CHUNKS + 1 + i]
        )
        for i in range(2)
    ]
    for copy in edges:
        copy.start(priority=1)
    for i in range(1, TOP):
        pltpu.make_async_copy(top_in.at[pl.ds(i * WIDTH, WIDTH)], blocks.at[i], load_sem.at[i]).start(priority=1)
    rest = [
        pltpu.make_async_copy(outer_in, blocks.at[MIDDLE, pl.ds(0, 256)], load_sem.at[MIDDLE]),
        pltpu.make_async_copy(mid_in, blocks.at[MIDDLE, pl.ds(256, 128)], load_sem.at[CHUNKS]),
        pltpu.make_async_copy(leaf_in.at[pl.ds(0, 512)], blocks.at[LEAF], load_sem.at[LEAF]),
        pltpu.make_async_copy(leaf_in.at[pl.ds(512, 448)], blocks.at[LEAF + 1, pl.ds(0, 448)], load_sem.at[LEAF + 1]),
    ]
    for copy in rest:
        copy.start(priority=1)

    barrier = pltpu.get_barrier_semaphore()

    @pl.loop(1, PLANE)
    def _(step):
        other = lax.rem(me + step, PLANE)
        pl.semaphore_signal(barrier, inc=1, device_id={"gy": other // RING, "gz": lax.rem(other, RING)})

    @pl.loop(1, GX)
    def _(step):
        pl.semaphore_signal(barrier, inc=1, device_id={"gx": lax.rem(gx + step, GX)})

    blocks[MIDDLE, pl.ds(384, 128)] = jnp.zeros((128, ROWS), F32)
    blocks[LEAF + 1, pl.ds(448, 64)] = jnp.zeros((64, ROWS), F32)
    for copy in smalls:
        copy.wait()
    ordered[...] = stacked(permuted(rhs[...], order[...]))

    turn = gy + gz + 2 * depth
    late, early = turn >= LATE, turn <= EARLY
    between = jnp.logical_not(late | early)
    latest = turn >= LATEST
    last = depth == RING - 1

    def enter():
        pl.semaphore_wait(barrier, PLANE - 1 + GX - 1)

    def send_half(chunk, k):
        owner = 2 * depth_of(chunk) + k

        @pl.when(owner != gx)
        def _():
            pltpu.make_async_remote_copy(
                src_ref=part.at[pl.ds(PIECES * chunk + HALF * k, HALF)],
                dst_ref=gx_recv.at[lax.rem(gx - owner + GX, GX)],
                send_sem=send_sem.at[0],
                recv_sem=recv_sem.at[0],
                device_id={"gx": owner},
            ).start()

    def send_chunk(chunk):
        send_half(chunk, 0)
        send_half(chunk, 1)

    def send_ring():
        ring_send[...] = part[pl.ds(PIECES * MIDDLE, 3)]
        for step in range(1, RING):
            pltpu.make_async_remote_copy(
                src_ref=ring_send,
                dst_ref=mid_recv.at[RING - step],
                send_sem=send_sem.at[1],
                recv_sem=recv_sem.at[1],
                device_id={"gz": lax.rem(gz + step, RING)},
            ).start()

    def exchange_plane():
        wait_for(gx_recv.at[pl.ds(1, GX - 1)], recv_sem.at[0])
        plane_recv[me] = part[pl.ds(mine, HALF)] + jnp.sum(gx_recv[pl.ds(1, GX - 1)], axis=0)

        @pl.loop(0, PLANE)
        def _(other):
            @pl.when(other != me)
            def _():
                pltpu.make_async_remote_copy(
                    src_ref=plane_recv.at[me],
                    dst_ref=plane_recv.at[me],
                    send_sem=send_sem.at[2],
                    recv_sem=recv_sem.at[2],
                    device_id={"gy": other // RING, "gz": lax.rem(other, RING)},
                ).start()

    def exchange_gy():
        wait_for(mid_recv.at[pl.ds(1, RING - 1)], recv_sem.at[1])
        ring_total[...] = ring_send[...] + jnp.sum(mid_recv[pl.ds(1, RING - 1)], axis=0)
        for step in range(1, RING):
            pltpu.make_async_remote_copy(
                src_ref=ring_total.at[pl.ds(0, 2)],
                dst_ref=outer_recv.at[RING - step],
                send_sem=send_sem.at[3],
                recv_sem=recv_sem.at[3],
                device_id={"gy": lax.rem(gy + step, RING)},
            ).start()

    def after_top():
        exchange_plane()
        pl.when(depth < RING - 1)(exchange_gy)

    def gather_sums(chunk, start, width):
        high, low = halves(blocks[chunk, pl.ds(start, width)])
        split[chunk, pl.ds(start, width)] = high
        split[chunk, pl.ds(WIDTH + start, width)] = low
        sums = folded(collect(ordered[...], high) + collect(ordered[...], low))
        for k in range(width // LANES):
            part[PIECES * chunk + start // LANES + k] = sums[:, k * LANES : (k + 1) * LANES]

    edges[0].wait()
    gather_sums(0, 0, SIDE)

    @pl.loop(0, CHUNKS)
    def _(chunk):
        @pl.when((chunk > 0) & (chunk < TOP))
        def _():
            wait_for(blocks.at[chunk], load_sem.at[chunk])

        @pl.when((chunk == MIDDLE) & between)
        def _():
            enter()
            pl.loop(0, TOP)(send_chunk)

        @pl.when((chunk == MIDDLE) & last)
        def _():
            exchange_plane()

        @pl.when((chunk == LEAF) & jnp.logical_not(early | last))
        def _():
            after_top()

        @pl.when(chunk == MIDDLE)
        def _():
            rest[0].wait()
            rest[1].wait()

        @pl.when(chunk == LEAF)
        def _():
            rest[2].wait()

        @pl.when(chunk == LEAF + 1)
        def _():
            rest[3].wait()

        @pl.when(chunk > 0)
        def _():
            gather_sums(chunk, 0, WIDTH)

        @pl.when(chunk == 0)
        def _():
            edges[1].wait()
            gather_sums(0, SIDE, SIDE)

        @pl.when((chunk == 0) & latest)
        def _():
            enter()

        @pl.when((chunk == 1) & late & jnp.logical_not(latest))
        def _():
            enter()
            send_chunk(0)

        @pl.when((chunk < TOP) & late & ((chunk > 0) | latest))
        def _():
            send_chunk(chunk)

        @pl.when((chunk == MIDDLE) & jnp.logical_not(early))
        def _():
            send_ring()

    @pl.when(early)
    def _():
        enter()
        pl.loop(0, TOP)(send_chunk)
        send_ring()
        after_top()

    def twice(pieces):
        both = stacked(row(pieces))
        return row([both, both])

    leaf_weights = live(row([part[PIECES * LEAF + i] for i in range(2 * PIECES)]), live_leaf[0])
    leaf_weights = [leaf_weights[:, i * LANES : (i + 1) * LANES] for i in range(2 * PIECES)]
    result[...] = spread(
        row([twice(leaf_weights[:PIECES]), twice(leaf_weights[PIECES:])]),
        split[pl.ds(LEAF, 2)].reshape(4 * WIDTH, ROWS),
    )

    def total_copy(owner, other):
        piece = PIECES * chunk_of(owner // 2) + HALF * lax.rem(owner, 2)
        pieces = weights.at[pl.ds(piece, HALF)]
        return pltpu.make_async_remote_copy(
            src_ref=pieces,
            dst_ref=pieces,
            send_sem=send_sem.at[4],
            recv_sem=total_sem.at[owner],
            device_id={"gx": other},
        )

    def exchange_total():
        wait_for(plane_recv.at[pl.ds(0, PLANE - 1)], recv_sem.at[2])
        weights[pl.ds(mine, HALF)] = jnp.sum(plane_recv[...], axis=0)
        for other in range(GX):

            @pl.when(gx != other)
            def _():
                total_copy(gx, other).start()

    first = 1 - (depth + RING - 1) // RING

    @pl.loop(0, TOP + 1)
    def _(step):
        after = [(step + TOP - k) // TOP for k in range(TOP + 1)]
        chunk = step + first * (TOP - after[1] - 3 * after[2] + after[3] + after[4] - step)

        @pl.when(((step == 0) & (depth > 0)) | ((step == 1) & (depth == 0)))
        def _():
            exchange_total()

        @pl.when((step == 0) & (depth == RING - 1))
        def _():
            exchange_gy()

        @pl.when(chunk < TOP)
        def _():
            for k in range(2):
                owner = 2 * depth_of(chunk) + k

                @pl.when(owner != gx)
                def _():
                    total_copy(owner, gx).wait_recv()

        @pl.when(chunk == MIDDLE)
        def _():
            wait_for(outer_recv.at[pl.ds(1, RING - 1)], recv_sem.at[3])
            outer_total = ring_total[pl.ds(0, 2)] + jnp.sum(outer_recv[pl.ds(1, RING - 1)], axis=0)
            outer_weights = live(row([outer_total[0], outer_total[1]]), live_outer[0])
            weights[PIECES * MIDDLE] = outer_weights[:, :LANES]
            weights[PIECES * MIDDLE + 1] = outer_weights[:, LANES:]
            weights[PIECES * MIDDLE + 2] = live(ring_total[2], live_mid[0])
            weights[PIECES * MIDDLE + 3] = jnp.zeros((NRHS, LANES), F32)

        result[...] += spread(twice([weights[PIECES * chunk + k] for k in range(PIECES)]), split[chunk])

    out[...] = folded(result[...])

    wait_for(gx_recv.at[pl.ds(1, GX - 1)], send_sem.at[0])
    wait_for(mid_recv.at[pl.ds(1, RING - 1)], send_sem.at[1])
    wait_for(plane_recv.at[pl.ds(0, PLANE - 1)], send_sem.at[2])
    wait_for(outer_recv.at[pl.ds(1, RING - 1)], send_sem.at[3])
    wait_for(gx_recv.at[pl.ds(1, GX - 1)], send_sem.at[4])


def local(rhs, row_order, x_top, x_outer, x_mid, x_leaf, live_outer, live_mid, live_leaf):
    piece = (NRHS, LANES)
    call = pl.pallas_call(
        kernel,
        out_shape=jax.ShapeDtypeStruct((NRHS, ROWS), F32),
        in_specs=[pl.BlockSpec(memory_space=pltpu.HBM)] * 6 + [pl.BlockSpec(memory_space=pl.ANY)] * 3,
        out_specs=pl.BlockSpec(memory_space=pltpu.VMEM),
        scratch_shapes=[
            pltpu.SMEM((1,), jnp.int32),
            pltpu.SMEM((1,), jnp.int32),
            pltpu.SMEM((1,), jnp.int32),
            pltpu.VMEM((NRHS, ROWS), F32),
            pltpu.VMEM((ROWS // LANES, LANES), jnp.int32),
            pltpu.VMEM((CHUNKS, WIDTH, ROWS), F32),
            pltpu.VMEM((CHUNKS, 2 * WIDTH, ROWS), BF16),
            pltpu.VMEM((2 * NRHS, ROWS), BF16),
            pltpu.VMEM((PIECES * CHUNKS, *piece), F32),
            pltpu.VMEM((PIECES * (TOP + 1), *piece), F32),
            pltpu.VMEM((2 * NRHS, ROWS), F32),
            pltpu.VMEM((GX, HALF, *piece), F32),
            pltpu.VMEM((PLANE, HALF, *piece), F32),
            pltpu.VMEM((3, *piece), F32),
            pltpu.VMEM((RING, 3, *piece), F32),
            pltpu.VMEM((3, *piece), F32),
            pltpu.VMEM((RING, 2, *piece), F32),
            pltpu.SemaphoreType.DMA((CHUNKS + 3,)),
            pltpu.SemaphoreType.DMA((5,)),
            pltpu.SemaphoreType.DMA((5,)),
            pltpu.SemaphoreType.DMA((4,)),
            pltpu.SemaphoreType.DMA((GX,)),
        ],
        compiler_params=pltpu.CompilerParams(
            collective_id=0, has_side_effects=True, vmem_limit_bytes=48 * 1024 * 1024
        ),
        cost_estimate=pl.CostEstimate(flops=2 * 4 * 8 * 1024 * 3392, bytes_accessed=3392 * 4096, transcendentals=0),
        name="xxt",
    )
    large = (rhs, row_order.reshape(ROWS // LANES, LANES), x_top, x_outer, x_mid, x_leaf)
    large = [pltpu.with_memory_space_constraint(operand, pltpu.HBM) for operand in large]
    return call(*large, live_outer, live_mid, live_leaf)


def solution(mesh):
    return jax.shard_map(
        local,
        mesh=mesh,
        in_specs=(
            P(None, ("gx", "gy", "gz")),
            P(("gx", "gy", "gz")),
            P(None, ("gx", "gy", "gz")),
            P(None, ("gx", "gy", "gz")),
            P(None, ("gx", "gy", "gz")),
            P(None, ("gx", "gy", "gz")),
            P("gx"),
            P(("gx", "gy")),
            P(("gx", "gy", "gz")),
        ),
        out_specs=P(None, ("gx", "gy", "gz")),
        check_vma=False,
    )
```

```python
import jax
import jax.numpy as jnp
from jax import lax
from jax.experimental import pallas as pl
from jax.experimental.pallas import tpu as pltpu
from jax.sharding import PartitionSpec as P

F32 = jnp.float32
BF16 = jnp.bfloat16
LANES = 128
NRHS = 8
ROWS = 1024
WIDTH = 512
PIECES = WIDTH // LANES
HALF = PIECES // 2
SIDE = WIDTH // 2
TOP = 4
MIDDLE = 4
LEAF = 5
CHUNKS = 7
PLANE = 16
GX = 8
RING = 4
LATE = 3
LATEST = 11
EARLY = 1


def halves(values):
    high = values.astype(BF16)
    return high, (values - high.astype(F32)).astype(BF16)


def stacked(values):
    high = values.astype(BF16).astype(F32)
    return jnp.concatenate([high, values - high], axis=0).astype(BF16)


def folded(values):
    return values[:NRHS] + values[NRHS:]


def permuted(rhs, order):
    out = []
    for j in range(ROWS // LANES):
        place = jnp.broadcast_to(order[j : j + 1, :], (NRHS, LANES))
        lane, block = place % LANES, place // LANES
        taken = jnp.zeros((NRHS, LANES), F32)
        for s in range(ROWS // LANES):
            source = rhs[:, s * LANES : (s + 1) * LANES]
            taken = jnp.where(block == s, jnp.take_along_axis(source, lane, axis=1), taken)
        out.append(taken)
    return jnp.concatenate(out, axis=1)


def collect(ordered, blocks):
    return lax.dot_general(ordered, blocks, (((1,), (1,)), ((), ())), preferred_element_type=F32)


def spread(weights, blocks):
    return lax.dot_general(weights, blocks, (((1,), (0,)), ((), ())), preferred_element_type=F32)


def row(pieces):
    return jnp.concatenate(pieces, axis=1)


def live(values, count):
    return jnp.where(lax.broadcasted_iota(jnp.int32, values.shape, 1) < count, values, jnp.float32(0.0))


def depth_of(chunk):
    high, low = chunk // 2, lax.rem(chunk, 2)
    return 2 - low + high - 2 * high * low


def chunk_of(depth):
    high, low = depth // 2, lax.rem(depth, 2)
    return 3 - 2 * low - 3 * high + 4 * high * low


def wait_for(ref, sem):
    pltpu.make_async_copy(ref, ref, sem).wait()


def kernel(
    rhs_in, order_in, top_in, outer_in, mid_in, leaf_in, live_outer_in, live_mid_in, live_leaf_in, out,
    live_outer, live_mid, live_leaf,
    rhs, order, blocks, split, ordered, part, weights, result,
    gx_recv, plane_recv, ring_send, mid_recv, ring_total, outer_recv,
    load_sem, small_sem, send_sem, recv_sem, total_sem,
):
    gx, gy, gz = lax.axis_index("gx"), lax.axis_index("gy"), lax.axis_index("gz")
    me = gy * RING + gz
    depth, core = gx // 2, lax.rem(gx, 2)
    mine = PIECES * chunk_of(depth) + HALF * core
    smalls = [
        pltpu.make_async_copy(rhs_in, rhs, small_sem.at[0]),
        pltpu.make_async_copy(order_in, order, small_sem.at[1]),
        pltpu.make_async_copy(live_outer_in, live_outer, small_sem.at[2]),
        pltpu.make_async_copy(live_mid_in, live_mid, small_sem.at[3]),
        pltpu.make_async_copy(live_leaf_in, live_leaf, small_sem.at[4]),
    ]
    for copy in smalls:
        copy.start()
    edges = [
        pltpu.make_async_copy(
            top_in.at[pl.ds(i * SIDE, SIDE)], blocks.at[0, pl.ds(i * SIDE, SIDE)], load_sem.at[CHUNKS + 1 + i]
        )
        for i in range(2)
    ]
    for copy in edges:
        copy.start(priority=1)
    for i in range(1, TOP):
        pltpu.make_async_copy(top_in.at[pl.ds(i * WIDTH, WIDTH)], blocks.at[i], load_sem.at[i]).start(priority=1)
    rest = [
        pltpu.make_async_copy(outer_in, blocks.at[MIDDLE, pl.ds(0, 256)], load_sem.at[MIDDLE]),
        pltpu.make_async_copy(mid_in, blocks.at[MIDDLE, pl.ds(256, 128)], load_sem.at[CHUNKS]),
        pltpu.make_async_copy(leaf_in.at[pl.ds(0, 512)], blocks.at[LEAF], load_sem.at[LEAF]),
        pltpu.make_async_copy(leaf_in.at[pl.ds(512, 448)], blocks.at[LEAF + 1, pl.ds(0, 448)], load_sem.at[LEAF + 1]),
    ]
    for copy in rest:
        copy.start(priority=1)

    barrier = pltpu.get_barrier_semaphore()

    @pl.loop(1, PLANE)
    def _(step):
        other = lax.rem(me + step, PLANE)
        pl.semaphore_signal(barrier, inc=1, device_id={"gy": other // RING, "gz": lax.rem(other, RING)})

    @pl.loop(1, GX)
    def _(step):
        pl.semaphore_signal(barrier, inc=1, device_id={"gx": lax.rem(gx + step, GX)})

    blocks[MIDDLE, pl.ds(384, 128)] = jnp.zeros((128, ROWS), F32)
    blocks[LEAF + 1, pl.ds(448, 64)] = jnp.zeros((64, ROWS), F32)
    for copy in smalls:
        copy.wait()
    ordered[...] = stacked(permuted(rhs[...], order[...]))

    turn = gy + gz + 2 * depth
    late, early = turn >= LATE, turn <= EARLY
    between = jnp.logical_not(late | early)
    latest = turn >= LATEST
    last = depth == RING - 1

    def enter():
        pl.semaphore_wait(barrier, PLANE - 1 + GX - 1)

    def send_half(chunk, k):
        owner = 2 * depth_of(chunk) + k

        @pl.when(owner != gx)
        def _():
            pltpu.make_async_remote_copy(
                src_ref=part.at[pl.ds(PIECES * chunk + HALF * k, HALF)],
                dst_ref=gx_recv.at[lax.rem(gx - owner + GX, GX)],
                send_sem=send_sem.at[0],
                recv_sem=recv_sem.at[0],
                device_id={"gx": owner},
            ).start()

    def send_chunk(chunk):
        send_half(chunk, 0)
        send_half(chunk, 1)

    def send_ring():
        ring_send[...] = part[pl.ds(PIECES * MIDDLE, 3)]
        for step in range(1, RING):
            pltpu.make_async_remote_copy(
                src_ref=ring_send,
                dst_ref=mid_recv.at[RING - step],
                send_sem=send_sem.at[1],
                recv_sem=recv_sem.at[1],
                device_id={"gz": lax.rem(gz + step, RING)},
            ).start()

    def exchange_plane():
        wait_for(gx_recv.at[pl.ds(1, GX - 1)], recv_sem.at[0])
        plane_recv[me] = part[pl.ds(mine, HALF)] + jnp.sum(gx_recv[pl.ds(1, GX - 1)], axis=0)

        @pl.loop(0, PLANE)
        def _(other):
            @pl.when(other != me)
            def _():
                pltpu.make_async_remote_copy(
                    src_ref=plane_recv.at[me],
                    dst_ref=plane_recv.at[me],
                    send_sem=send_sem.at[2],
                    recv_sem=recv_sem.at[2],
                    device_id={"gy": other // RING, "gz": lax.rem(other, RING)},
                ).start()

    def exchange_gy():
        wait_for(mid_recv.at[pl.ds(1, RING - 1)], recv_sem.at[1])
        ring_total[...] = ring_send[...] + jnp.sum(mid_recv[pl.ds(1, RING - 1)], axis=0)
        for step in range(1, RING):
            pltpu.make_async_remote_copy(
                src_ref=ring_total.at[pl.ds(0, 2)],
                dst_ref=outer_recv.at[RING - step],
                send_sem=send_sem.at[3],
                recv_sem=recv_sem.at[3],
                device_id={"gy": lax.rem(gy + step, RING)},
            ).start()

    def after_top():
        exchange_plane()
        pl.when(depth < RING - 1)(exchange_gy)

    def gather_sums(chunk, start, width):
        high, low = halves(blocks[chunk, pl.ds(start, width)])
        split[chunk, pl.ds(start, width)] = high
        split[chunk, pl.ds(WIDTH + start, width)] = low
        sums = folded(collect(ordered[...], high) + collect(ordered[...], low))
        for k in range(width // LANES):
            part[PIECES * chunk + start // LANES + k] = sums[:, k * LANES : (k + 1) * LANES]

    edges[0].wait()
    gather_sums(0, 0, SIDE)

    @pl.loop(0, CHUNKS)
    def _(chunk):
        @pl.when((chunk > 0) & (chunk < TOP))
        def _():
            wait_for(blocks.at[chunk], load_sem.at[chunk])

        @pl.when((chunk == MIDDLE) & between)
        def _():
            enter()
            pl.loop(0, TOP)(send_chunk)

        @pl.when((chunk == MIDDLE) & last)
        def _():
            exchange_plane()

        @pl.when((chunk == LEAF) & jnp.logical_not(early | last))
        def _():
            after_top()

        @pl.when(chunk == MIDDLE)
        def _():
            rest[0].wait()
            rest[1].wait()

        @pl.when(chunk == LEAF)
        def _():
            rest[2].wait()

        @pl.when(chunk == LEAF + 1)
        def _():
            rest[3].wait()

        @pl.when(chunk > 0)
        def _():
            gather_sums(chunk, 0, WIDTH)

        @pl.when(chunk == 0)
        def _():
            edges[1].wait()
            gather_sums(0, SIDE, SIDE)

        @pl.when((chunk == 0) & latest)
        def _():
            enter()

        @pl.when((chunk == 1) & late & jnp.logical_not(latest))
        def _():
            enter()
            send_chunk(0)

        @pl.when((chunk < TOP) & late & ((chunk > 0) | latest))
        def _():
            send_chunk(chunk)

        @pl.when((chunk == MIDDLE) & jnp.logical_not(early))
        def _():
            send_ring()

    @pl.when(early)
    def _():
        enter()
        pl.loop(0, TOP)(send_chunk)
        send_ring()
        after_top()

    def twice(pieces):
        both = stacked(row(pieces))
        return row([both, both])

    leaf_weights = live(row([part[PIECES * LEAF + i] for i in range(2 * PIECES)]), live_leaf[0])
    leaf_weights = [leaf_weights[:, i * LANES : (i + 1) * LANES] for i in range(2 * PIECES)]
    result[...] = spread(
        row([twice(leaf_weights[:PIECES]), twice(leaf_weights[PIECES:])]),
        split[pl.ds(LEAF, 2)].reshape(4 * WIDTH, ROWS),
    )

    def total_copy(owner, other):
        piece = PIECES * chunk_of(owner // 2) + HALF * lax.rem(owner, 2)
        pieces = weights.at[pl.ds(piece, HALF)]
        return pltpu.make_async_remote_copy(
            src_ref=pieces,
            dst_ref=pieces,
            send_sem=send_sem.at[4],
            recv_sem=total_sem.at[owner],
            device_id={"gx": other},
        )

    def exchange_total():
        wait_for(plane_recv.at[pl.ds(0, PLANE - 1)], recv_sem.at[2])
        weights[pl.ds(mine, HALF)] = jnp.sum(plane_recv[...], axis=0)
        for other in range(GX):

            @pl.when(gx != other)
            def _():
                total_copy(gx, other).start()

    first = 1 - (depth + RING - 1) // RING

    @pl.loop(0, TOP + 1)
    def _(step):
        after = [(step + TOP - k) // TOP for k in range(TOP + 1)]
        chunk = step + first * (TOP - after[1] - 3 * after[2] + after[3] + after[4] - step)

        @pl.when(((step == 0) & (depth > 0)) | ((step == 1) & (depth == 0)))
        def _():
            exchange_total()

        @pl.when((step == 0) & (depth == RING - 1))
        def _():
            exchange_gy()

        @pl.when(chunk < TOP)
        def _():
            for k in range(2):
                owner = 2 * depth_of(chunk) + k

                @pl.when(owner != gx)
                def _():
                    total_copy(owner, gx).wait_recv()

        @pl.when(chunk == MIDDLE)
        def _():
            wait_for(outer_recv.at[pl.ds(1, RING - 1)], recv_sem.at[3])
            outer_total = ring_total[pl.ds(0, 2)] + jnp.sum(outer_recv[pl.ds(1, RING - 1)], axis=0)
            outer_weights = live(row([outer_total[0], outer_total[1]]), live_outer[0])
            weights[PIECES * MIDDLE] = outer_weights[:, :LANES]
            weights[PIECES * MIDDLE + 1] = outer_weights[:, LANES:]
            weights[PIECES * MIDDLE + 2] = live(ring_total[2], live_mid[0])
            weights[PIECES * MIDDLE + 3] = jnp.zeros((NRHS, LANES), F32)

        result[...] += spread(twice([weights[PIECES * chunk + k] for k in range(PIECES)]), split[chunk])

    out[...] = folded(result[...])

    wait_for(gx_recv.at[pl.ds(1, GX - 1)], send_sem.at[0])
    wait_for(mid_recv.at[pl.ds(1, RING - 1)], send_sem.at[1])
    wait_for(plane_recv.at[pl.ds(0, PLANE - 1)], send_sem.at[2])
    wait_for(outer_recv.at[pl.ds(1, RING - 1)], send_sem.at[3])
    wait_for(gx_recv.at[pl.ds(1, GX - 1)], send_sem.at[4])


def local(rhs, row_order, x_top, x_outer, x_mid, x_leaf, live_outer, live_mid, live_leaf):
    piece = (NRHS, LANES)
    call = pl.pallas_call(
        kernel,
        out_shape=jax.ShapeDtypeStruct((NRHS, ROWS), F32),
        in_specs=[pl.BlockSpec(memory_space=pltpu.HBM)] * 6 + [pl.BlockSpec(memory_space=pl.ANY)] * 3,
        out_specs=pl.BlockSpec(memory_space=pltpu.VMEM),
        scratch_shapes=[
            pltpu.SMEM((1,), jnp.int32),
            pltpu.SMEM((1,), jnp.int32),
            pltpu.SMEM((1,), jnp.int32),
            pltpu.VMEM((NRHS, ROWS), F32),
            pltpu.VMEM((ROWS // LANES, LANES), jnp.int32),
            pltpu.VMEM((CHUNKS, WIDTH, ROWS), F32),
            pltpu.VMEM((CHUNKS, 2 * WIDTH, ROWS), BF16),
            pltpu.VMEM((2 * NRHS, ROWS), BF16),
            pltpu.VMEM((PIECES * CHUNKS, *piece), F32),
            pltpu.VMEM((PIECES * (TOP + 1), *piece), F32),
            pltpu.VMEM((2 * NRHS, ROWS), F32),
            pltpu.VMEM((GX, HALF, *piece), F32),
            pltpu.VMEM((PLANE, HALF, *piece), F32),
            pltpu.VMEM((3, *piece), F32),
            pltpu.VMEM((RING, 3, *piece), F32),
            pltpu.VMEM((3, *piece), F32),
            pltpu.VMEM((RING, 2, *piece), F32),
            pltpu.SemaphoreType.DMA((CHUNKS + 3,)),
            pltpu.SemaphoreType.DMA((5,)),
            pltpu.SemaphoreType.DMA((5,)),
            pltpu.SemaphoreType.DMA((4,)),
            pltpu.SemaphoreType.DMA((GX,)),
        ],
        compiler_params=pltpu.CompilerParams(
            collective_id=0, has_side_effects=True, vmem_limit_bytes=48 * 1024 * 1024
        ),
        cost_estimate=pl.CostEstimate(flops=2 * 4 * 8 * 1024 * 3392, bytes_accessed=3392 * 4096, transcendentals=0),
        name="xxt",
    )
    large = (rhs, row_order.reshape(ROWS // LANES, LANES), x_top, x_outer, x_mid, x_leaf)
    large = [pltpu.with_memory_space_constraint(operand, pltpu.HBM) for operand in large]
    return call(*large, live_outer, live_mid, live_leaf)


def solution(mesh):
    return jax.shard_map(
        local,
        mesh=mesh,
        in_specs=(
            P(None, ("gx", "gy", "gz")),
            P(("gx", "gy", "gz")),
            P(None, ("gx", "gy", "gz")),
            P(None, ("gx", "gy", "gz")),
            P(None, ("gx", "gy", "gz")),
            P(None, ("gx", "gy", "gz")),
            P("gx"),
            P(("gx", "gy")),
            P(("gx", "gy", "gz")),
        ),
        out_specs=P(None, ("gx", "gy", "gz")),
        check_vma=False,
    )
```
